128 devices in a mesh: mod: 16 (over z, y_hi, core), ex: 8 (over y_lo, x).
Axes of the slice: x: 4, y: 4 (y_hi: 2, y_lo: 2; y = y_hi * 2 + y_lo), z: 4, core: 2. Of those that a mesh axis runs over, the one named last changes fastest.
Arguments:
- queries: bfloat16 [512, 16, 4096], P(('mod', 'ex')), may hold values from -6 to 6
- hessian_inv: bfloat16 [16, 4096, 4096], P('mod', 'ex'), may hold values from -1 to 5
- train_sketch: bfloat16 [16384, 16, 4096], P('ex', 'mod'), may hold values from -0.0234375 to 0.0234375
- module_slot: int32 [16], replicated, may hold values from 0 to 15, each once
- arrival_of: int32 [512], replicated, may hold values from 0 to 511, each once
Outputs:
- scores: float32 [512, 16384], P('mod', 'ex')
The draws below stay inside these ranges and needn't reach their ends.
Inputs may be any that keep to these rules, and one draw needn't show every extreme that they name: Slot k holds module module_slot[k]; every module is held once. Query k stands in row arrival_of[k] of queries; every row holds one query.
All inputs are finite; a program needn't handle non-finite values.
Results may differ from the reference program's by a relative error of at most 0.0029.
Values may be sent and summed in bfloat16 or wider, within the bound.
No kernel may reach another device: no remote copies, remote signals or barrier semaphores. Data moves between devices by JAX's collectives and lax.ppermute only.
A program may use at most 256 MiB of HBM per device.

```python
import math
import jax
import jax.numpy as jnp
from jax import lax

S = 4096
M = 16
Q = 512
N = 16384


def draw_hessian_inv(key, part):
    key = jax.random.fold_in(key, 11)
    first, second = jax.random.split(key)
    diagonal = jnp.exp(jax.random.uniform(first, (M, S, 1), jnp.float32, math.log(0.5), math.log(2.0)))
    noise = jnp.clip(jax.random.normal(second, (M, S, S), jnp.float32), -6.0, 6.0) * (0.5 / math.sqrt(S))
    rowpos = lax.broadcasted_iota(jnp.int32, (S, S), 0)
    colpos = lax.broadcasted_iota(jnp.int32, (S, S), 1)
    return (noise + jnp.where(rowpos == colpos, diagonal, 0.0)).astype(jnp.bfloat16)


def block_scale(stream_key, dims, cuts, low, top_value):
    gain = 1.0
    for dim, parts in cuts:
        steps = jax.random.uniform(jax.random.fold_in(jax.random.fold_in(stream_key, 6), dim), (parts,), jnp.float32, low / len(cuts), top_value / len(cuts))
        gain = gain * jnp.repeat(jnp.exp(steps), dims[dim] // parts).reshape((-1,) + (1,) * (len(dims) - 1 - dim))
    return gain


def scatter_about(rng, shape, spread, limit, shards=(), kind=jnp.bfloat16):
    loudness = block_scale(rng, shape, shards, -0.22, 0.18) if shards else 1.0
    drawn = jax.random.normal(rng, shape, jnp.float32) * spread * loudness
    return jnp.minimum(jnp.maximum(drawn, -limit), limit).astype(kind)


def setup_inputs(seed: int = 0) -> dict:
    splits = jax.random.split(jax.random.key(seed), 6)
    queries = scatter_about(splits[0], (Q, M, S), 1.0, 6.0, ((0, 128),))
    hessian_inv = draw_hessian_inv(jax.random.fold_in(splits[5], 71), 0)
    train_sketch = scatter_about(splits[2], (N, M, S), (M * S) ** -0.5, 0.0234375, ((0, 8), (1, 16)))
    module_slot = jax.random.permutation(splits[3], M).astype(jnp.int32)
    arrival_of = jax.random.permutation(splits[4], Q).astype(jnp.int32)
    return {"queries": queries, "hessian_inv": hessian_inv, "train_sketch": train_sketch, "module_slot": module_slot, "arrival_of": arrival_of}


def reference(queries, hessian_inv, train_sketch, module_slot, arrival_of):
    slotted = jnp.take(queries, module_slot.astype(jnp.int32), axis=1)
    ordered = jnp.take(slotted, arrival_of.astype(jnp.int32), axis=0)

    def one_module(total, index):
        block = lax.dynamic_index_in_dim(hessian_inv, index, 0, keepdims=False)
        rows = lax.dynamic_index_in_dim(ordered, index, 1, keepdims=False)
        sketch = lax.dynamic_index_in_dim(train_sketch, index, 1, keepdims=False)
        precond = lax.dot_general(rows, block, (((1,), (1,)), ((), ())), preferred_element_type=jnp.float32).astype(jnp.bfloat16)
        added = lax.dot_general(precond, sketch, (((1,), (1,)), ((), ())), preferred_element_type=jnp.float32)
        return total + added, None

    total, _ = lax.scan(one_module, jnp.zeros((Q, N), jnp.float32), jnp.arange(M, dtype=jnp.int32))
    return total
```

```python
import jax
import jax.numpy as jnp
from jax import lax
from jax.experimental import pallas as pl
from jax.experimental.pallas import tpu as pltpu
from jax.sharding import PartitionSpec as P

AXES = ("mod", "ex")
NT = (((1,), (1,)), ((), ()))
VMEM = 12 * 1024 * 1024


def pairs(x=0, yl=0, z=0, yh=0, c=0, only=None):
    out = []
    for mod in range(16):
        for ex in range(8):
            if only is not None and mod % 2 not in only:
                continue
            core = mod % 2
            dyh = yh[core] if isinstance(yh, tuple) else yh
            to_mod = ((mod // 4 + z) % 4) * 4 + ((mod // 2 % 2) ^ dyh) * 2 + (core ^ c)
            to_ex = ((ex // 4) ^ yl) * 4 + (ex % 4 + x) % 4
            out.append((mod * 8 + ex, to_mod * 8 + to_ex))
    return out


def move(a, **offset):
    return lax.ppermute(a, AXES, pairs(**offset))


def spread(own):
    half = own.shape[0] // 2
    right = move(own, x=1)
    left = move(own, x=-1)
    across = move(own, yl=1)
    right, left, across = lax.optimization_barrier((right, left, across))
    far0 = move(right[:half], x=1)
    far1 = move(left[half:], x=-1)
    across_right = move(across, x=1)
    across_left = move(across, x=-1)
    corner0 = move(far0, yl=1)
    corner1 = move(far1, yl=1)
    return (own, right, left, across), (far0, far1, across_right, across_left, corner0, corner1)


def rows_of(blocks):
    return blocks[0][...] if len(blocks) == 1 else jnp.concatenate([b[...] for b in blocks], axis=0)


def on_chip(kernel, out_shape, scalars, *args):
    specs = [pl.BlockSpec(memory_space=pltpu.SMEM)] * len(scalars) + [pl.BlockSpec(memory_space=pltpu.VMEM)] * len(args)
    return pl.pallas_call(
        kernel,
        in_specs=specs,
        out_specs=pl.BlockSpec(memory_space=pltpu.VMEM),
        out_shape=out_shape,
        compiler_params=pltpu.CompilerParams(vmem_limit_bytes=VMEM),
        cost_estimate=pl.CostEstimate(flops=1, bytes_accessed=1, transcendentals=0),
    )(*scalars, *args)


def precondition(blocks, h):
    def kernel(*refs):
        *blocks, h, out = refs
        out[...] = lax.dot_general(rows_of(blocks), h[...], NT, preferred_element_type=jnp.float32).astype(out.dtype)

    rows = sum(b.shape[0] for b in blocks)
    return on_chip(kernel, jax.ShapeDtypeStruct((rows, 512), jnp.bfloat16), (), *blocks, h)


def precondition_order(blocks, h, first, place):
    def kernel(*refs):
        *blocks, h, first, place, out = refs
        rest = lax.dot_general(rows_of(blocks), h[...], NT, preferred_element_type=jnp.float32).astype(out.dtype)
        both = jnp.concatenate([first[...], rest], axis=0)
        at = lax.broadcasted_iota(jnp.int32, (512, 512), 0)
        pick = (place[...] == at).astype(both.dtype)
        out[...] = lax.dot_general(
            pick, both, (((0,), (0,)), ((), ())), preferred_element_type=jnp.float32
        ).astype(out.dtype)

    return on_chip(kernel, jax.ShapeDtypeStruct((512, 512), jnp.bfloat16), (), *blocks, h, first, place)


def score_near(blocks, near_slots, far_slots, sketch):
    total, tile = sketch.shape[0], 1024
    steps = total // tile

    def kernel(near_slots, far_slots, *refs):
        blocks, sketch, out, later, now, now_sem, later_sem = refs[:4], *refs[4:]

        def columns(slots, j):
            return pl.ds(pl.multiple_of(slots[j] * 512, 512), 512)

        fetch = [
            [
                pltpu.make_async_copy(
                    sketch.at[pl.ds(i * tile, tile), columns(near_slots, j)],
                    now.at[j, pl.ds(i * tile, tile)],
                    now_sem.at[i, j],
                )
                for j in range(4)
            ]
            for i in range(steps)
        ]
        ahead = [
            pltpu.make_async_copy(sketch.at[:, columns(far_slots, j)], later.at[j], later_sem.at[j]) for j in range(4)
        ]
        for copy in sum(fetch, []) + ahead:
            copy.start()
        for i in range(steps):
            terms = []
            for j in range(4):
                fetch[i][j].wait()
                terms.append(
                    lax.dot_general(
                        blocks[j][...], now[j, i * tile : i * tile + tile], NT, preferred_element_type=jnp.float32
                    )
                )
            out[:, i * tile : i * tile + tile] = sum(terms[1:], terms[0])
        for copy in ahead:
            copy.wait()

    smem, vmem = pl.BlockSpec(memory_space=pltpu.SMEM), pl.BlockSpec(memory_space=pltpu.VMEM)
    return pl.pallas_call(
        kernel,
        in_specs=[smem, smem, vmem, vmem, vmem, vmem, pl.BlockSpec(memory_space=pl.ANY)],
        out_specs=[vmem, vmem],
        out_shape=[
            jax.ShapeDtypeStruct((512, total), jnp.float32),
            jax.ShapeDtypeStruct((4, total, 512), jnp.bfloat16),
        ],
        scratch_shapes=[
            pltpu.VMEM((4, total, 512), jnp.bfloat16),
            pltpu.SemaphoreType.DMA((steps, 4)),
            pltpu.SemaphoreType.DMA((4,)),
        ],
        compiler_params=pltpu.CompilerParams(vmem_limit_bytes=2 * VMEM),
        cost_estimate=pl.CostEstimate(flops=1, bytes_accessed=1, transcendentals=0),
    )(near_slots, far_slots, *blocks, sketch)


def score_far(blocks, sketch, half, dtype, base, tile=1024):
    total = sketch.shape[1]

    def part(ref, columns=slice(None)):
        if ref.shape[0] == 256:
            return ref[:, columns]
        return ref[half * 256 : half * 256 + 256, columns]

    def kernel(*refs):
        blocks, sketch, base, out = refs[:4], *refs[4:]
        for i in range(total // tile):
            at = slice(i * tile, i * tile + tile)
            terms = [
                lax.dot_general(part(blocks[j]), sketch[j, at], NT, preferred_element_type=jnp.float32)
                for j in range(4)
            ]
            out[:, at] = sum(terms, part(base, at)).astype(out.dtype)

    return on_chip(kernel, jax.ShapeDtypeStruct((256, total), dtype), (), *blocks, sketch, base)


def local(queries, hessian_inv, train_sketch, module_slot, arrival_of):
    mod, ex = lax.axis_index("mod"), lax.axis_index("ex")
    z, yh, c = mod // 4, mod // 2 % 2, mod % 2
    yl, x = ex // 4, ex % 4
    h, sketch = hessian_inv[0], train_sketch[:, 0]

    pick = (module_slot[:, None] == jnp.arange(16)[None, :]).astype(jnp.bfloat16)
    slotted = jnp.einsum("km,rmb->krb", pick, queries, preferred_element_type=jnp.float32).astype(jnp.bfloat16)
    own = lax.all_to_all(slotted, "mod", split_axis=0, concat_axis=0, tiled=True).reshape(64, 4096)

    arrival = arrival_of.reshape(4, 2, 2, 32)
    arrival = lax.dynamic_slice_in_dim(jnp.concatenate([arrival, arrival], axis=0), z, 4, axis=0)
    yhs = [jnp.where(yh == c, arrival[:, 1 - s], arrival[:, s]) for s in (0, 1)]
    row = jnp.stack([jnp.where(c == 0, yhs[s], yhs[s][:, ::-1]) for s in (0, 1)])
    row = jnp.stack([row[0], row[1][:, ::-1]]).reshape(1, 512)
    source = row // 4 % 8
    dx, dy = (source % 4 - x) % 4, (source // 4) ^ yl
    block = jnp.where(
        dy == 0,
        jnp.where(dx == 0, 0, jnp.where(dx == 3, 1, jnp.where(dx == 1, 2, 4))),
        jnp.where(dx == 0, 3, jnp.where(dx == 3, 5, jnp.where(dx == 1, 6, 7))),
    )
    place = block * 64 + (row // 32) * 4 + row % 4
    left, right, over = (x + 3) % 4, (x + 1) % 4, (x + 2) % 4
    here, there = yl * 4, (1 - yl) * 4
    near_slots = jnp.stack([here + x, here + left, here + right, there + x]).astype(jnp.int32)
    far_slots = jnp.stack([here + over, there + left, there + right, there + over]).astype(jnp.int32)
    own, place, near_slots, far_slots = lax.optimization_barrier((own, place, near_slots, far_slots))

    near, far = spread(own)
    first = precondition(near, h)
    ordered = precondition_order(far, h, first, place)

    near, far = spread(ordered)
    base, later = score_near(near, near_slots, far_slots, sketch)
    far0, far1, across_right, across_left, corner0, corner1 = lax.optimization_barrier(far)
    send = score_far((far0, across_right, across_left, corner0), later, 0, jnp.bfloat16, base)
    got = move(send, c=1)
    keep = score_far((far1, across_right, across_left, corner1), later, 1, jnp.float32, base)

    chip = keep + got.astype(jnp.float32)
    parts = chip.astype(jnp.bfloat16)
    arrived = [move(parts[64 * d : 64 * d + 64], z=d, yh=(0, 1)) for d in (1, 2, 3)]
    other = move(parts[:64], yh=(0, 1), only=(1,))
    total = jnp.where(c == 0, chip[:64], other.astype(jnp.float32))
    for a in arrived:
        total = total + a.astype(jnp.float32)
    return total[32:] + move(total[:32], c=1)


def solution(mesh):
    in_specs = (P(("mod", "ex"), None, None), P("mod", "ex", None), P("ex", "mod", None), P(), P())
    out_specs = P("mod", "ex")
    return jax.shard_map(local, mesh=mesh, in_specs=in_specs, out_specs=out_specs, check_vma=False)
```

```python
import jax
import jax.numpy as jnp
from jax import lax
from jax.experimental import pallas as pl
from jax.experimental.pallas import tpu as pltpu
from jax.sharding import PartitionSpec as P

AXES = ("mod", "ex")
NT = (((1,), (1,)), ((), ()))
VMEM = 12 * 1024 * 1024


def pairs(x=0, yl=0, z=0, yh=0, c=0, only=None):
    out = []
    for mod in range(16):
        for ex in range(8):
            if only is not None and mod % 2 not in only:
                continue
            core = mod % 2
            dyh = yh[core] if isinstance(yh, tuple) else yh
            to_mod = ((mod // 4 + z) % 4) * 4 + ((mod // 2 % 2) ^ dyh) * 2 + (core ^ c)
            to_ex = ((ex // 4) ^ yl) * 4 + (ex % 4 + x) % 4
            out.append((mod * 8 + ex, to_mod * 8 + to_ex))
    return out


def move(a, **offset):
    return lax.ppermute(a, AXES, pairs(**offset))


def spread(top, low, meanwhile=None):
    across = move(jnp.concatenate([top, low], axis=0), yl=1)
    right_top, left_low = move(top, x=1), move(low, x=-1)
    right_low, left_top = move(low, x=1), move(top, x=-1)
    right_top, left_low, meanwhile = lax.optimization_barrier((right_top, left_low, meanwhile))
    far0, far1 = move(right_top, x=1), move(left_low, x=-1)
    across, right_low, left_top = lax.optimization_barrier((across, right_low, left_top))
    across_right, across_left = move(across, x=1), move(across, x=-1)
    corner0, corner1 = move(far0, yl=1), move(far1, yl=1)
    near = (top, low, right_top, right_low, left_top, left_low, across)
    return near, (far0, far1, across_right, across_left, corner0, corner1), meanwhile


def rows_of(blocks):
    return blocks[0][...] if len(blocks) == 1 else jnp.concatenate([b[...] for b in blocks], axis=0)


def on_chip(kernel, out_shape, scalars, *args):
    specs = [pl.BlockSpec(memory_space=pltpu.SMEM)] * len(scalars) + [pl.BlockSpec(memory_space=pltpu.VMEM)] * len(args)
    return pl.pallas_call(
        kernel,
        in_specs=specs,
        out_specs=jax.tree.map(lambda _: pl.BlockSpec(memory_space=pltpu.VMEM), out_shape),
        out_shape=out_shape,
        compiler_params=pltpu.CompilerParams(vmem_limit_bytes=VMEM),
        cost_estimate=pl.CostEstimate(flops=1, bytes_accessed=1, transcendentals=0),
    )(*scalars, *args)


def precondition(blocks, h):
    def kernel(*refs):
        *blocks, h, out = refs
        out[...] = lax.dot_general(rows_of(blocks), h[...], NT, preferred_element_type=jnp.float32).astype(out.dtype)

    rows = sum(b.shape[0] for b in blocks)
    return on_chip(kernel, jax.ShapeDtypeStruct((rows, 512), jnp.bfloat16), (), *blocks, h)


def precondition_order(blocks, h, first, place):
    def kernel(*refs):
        *blocks, h, first, place, top, low = refs
        rest = lax.dot_general(rows_of(blocks), h[...], NT, preferred_element_type=jnp.float32).astype(top.dtype)
        both = jnp.concatenate([first[...], rest], axis=0)
        at = lax.broadcasted_iota(jnp.int32, (512, 512), 0)
        pick = (place[...] == at).astype(both.dtype)
        ordered = lax.dot_general(pick, both, (((0,), (0,)), ((), ())), preferred_element_type=jnp.float32)
        top[...] = ordered[:256].astype(top.dtype)
        low[...] = ordered[256:].astype(low.dtype)

    half = jax.ShapeDtypeStruct((256, 512), jnp.bfloat16)
    return on_chip(kernel, [half, half], (), *blocks, h, first, place)


def score_own(top, low, slots, sketch):
    total, tile = sketch.shape[0], 1024
    steps = total // tile

    def kernel(slots, top, low, sketch, out, later, now, now_sem, later_sem):
        def columns(j):
            return pl.ds(pl.multiple_of(slots[j] * 512, 512), 512)

        fetch = [
            pltpu.make_async_copy(
                sketch.at[pl.ds(i * tile, tile), columns(0)], now.at[pl.ds(i * tile, tile)], now_sem.at[i]
            )
            for i in range(steps)
        ]
        ahead = [pltpu.make_async_copy(sketch.at[:, columns(j + 1)], later.at[j], later_sem.at[j]) for j in range(7)]
        for copy in fetch + ahead:
            copy.start()
        rows = rows_of((top, low))
        for i in range(steps):
            fetch[i].wait()
            at = slice(i * tile, i * tile + tile)
            out[:, at] = lax.dot_general(rows, now[at], NT, preferred_element_type=jnp.float32)
        for copy in ahead:
            copy.wait()

    smem, vmem = pl.BlockSpec(memory_space=pltpu.SMEM), pl.BlockSpec(memory_space=pltpu.VMEM)
    return pl.pallas_call(
        kernel,
        in_specs=[smem, vmem, vmem, pl.BlockSpec(memory_space=pl.ANY)],
        out_specs=[vmem, vmem],
        out_shape=[
            jax.ShapeDtypeStruct((512, total), jnp.float32),
            jax.ShapeDtypeStruct((7, total, 512), jnp.bfloat16),
        ],
        scratch_shapes=[
            pltpu.VMEM((total, 512), jnp.bfloat16),
            pltpu.SemaphoreType.DMA((steps,)),
            pltpu.SemaphoreType.DMA((7,)),
        ],
        compiler_params=pltpu.CompilerParams(vmem_limit_bytes=28 * 1024 * 1024),
        cost_estimate=pl.CostEstimate(flops=1, bytes_accessed=1, transcendentals=0),
    )(slots, top, low, sketch)


def score_more(blocks, first, sketch, base, half=None, dtype=jnp.float32, tile=1024):
    total = sketch.shape[1]
    sizes = [len(b) for b in blocks]
    rows = 512 if half is None else 256

    def part(ref, columns=slice(None)):
        if ref.shape[0] == rows:
            return ref[:, columns]
        return ref[half * 256 : half * 256 + 256, columns]

    def kernel(*refs):
        held, (sketch, base, out) = list(refs[:-3]), refs[-3:]
        wholes = []
        for size in sizes:
            taken = [held.pop(0) for _ in range(size)]
            wholes.append(rows_of(taken) if size > 1 else part(taken[0]))
        for i in range(total // tile):
            at = slice(i * tile, i * tile + tile)
            terms = [
                lax.dot_general(w, sketch[first + j, at], NT, preferred_element_type=jnp.float32)
                for j, w in enumerate(wholes)
            ]
            out[:, at] = sum(terms, part(base, at)).astype(out.dtype)

    flat = [a for b in blocks for a in b]
    return on_chip(kernel, jax.ShapeDtypeStruct((rows, total), dtype), (), *flat, sketch, base)


def local(queries, hessian_inv, train_sketch, module_slot, arrival_of):
    mod, ex = lax.axis_index("mod"), lax.axis_index("ex")
    z, yh, c = mod // 4, mod // 2 % 2, mod % 2
    yl, x = ex // 4, ex % 4
    h, sketch = hessian_inv[0], train_sketch[:, 0]

    pick = (module_slot[:, None] == jnp.arange(16)[None, :]).astype(jnp.bfloat16)
    slotted = jnp.einsum("km,rmb->krb", pick, queries, preferred_element_type=jnp.float32).astype(jnp.bfloat16)
    own = lax.all_to_all(slotted, "mod", split_axis=0, concat_axis=0, tiled=True).reshape(64, 4096)

    arrival = arrival_of.reshape(4, 2, 2, 32)
    arrival = lax.dynamic_slice_in_dim(jnp.concatenate([arrival, arrival], axis=0), z, 4, axis=0)
    yhs = [jnp.where(yh == c, arrival[:, 1 - s], arrival[:, s]) for s in (0, 1)]
    row = jnp.stack([jnp.where(c == 0, yhs[s], yhs[s][:, ::-1]) for s in (0, 1)])
    row = jnp.stack([row[0], row[1][:, ::-1]]).reshape(1, 512)
    source = row // 4 % 8
    dx, dy = (source % 4 - x) % 4, (source // 4) ^ yl
    block = jnp.where(
        dy == 0,
        jnp.where(dx == 0, 0, jnp.where(dx == 3, 1, jnp.where(dx == 1, 2, 4))),
        jnp.where(dx == 0, 3, jnp.where(dx == 3, 5, jnp.where(dx == 1, 6, 7))),
    )
    place = block * 64 + (row // 32) * 4 + row % 4
    left, right, over = (x + 3) % 4, (x + 1) % 4, (x + 2) % 4
    here, there = yl * 4, (1 - yl) * 4
    slots = [here + x, here + left, here + right, there + x, here + over, there + left, there + right, there + over]
    own, place, slots = lax.optimization_barrier((own, place, jnp.stack(slots).astype(jnp.int32)))

    near, far, _ = spread(own[:32], own[32:])
    first = precondition(near, h)
    top, low = precondition_order(far, h, first, place)

    near, far, (base, later) = spread(top, low, score_own(top, low, slots, sketch))
    _, _, right_top, right_low, left_top, left_low, across = near
    far0, far1, *far = far
    base = score_more(((right_top, right_low), (left_top, left_low), (across,), (far0, far1)), 0, later, base)
    across_right, across_left, corner0, corner1 = lax.optimization_barrier(far)
    send = score_more(((across_right,), (across_left,), (corner0,)), 4, later, base, 0, jnp.bfloat16)
    got = move(send, c=1)
    keep = score_more(((across_right,), (across_left,), (corner1,)), 4, later, base, 1)

    chip = keep + got.astype(jnp.float32)
    parts = chip.astype(jnp.bfloat16)
    arrived = [move(parts[64 * d : 64 * d + 64], z=d, yh=(0, 1)) for d in (1, 2, 3)]
    other = move(parts[:64], yh=(0, 1), only=(1,))
    total = jnp.where(c == 0, chip[:64], other.astype(jnp.float32))
    for a in arrived:
        total = total + a.astype(jnp.float32)
    return total[32:] + move(total[:32], c=1)


def solution(mesh):
    in_specs = (P(("mod", "ex"), None, None), P("mod", "ex", None), P("ex", "mod", None), P(), P())
    out_specs = P("mod", "ex")
    return jax.shard_map(local, mesh=mesh, in_specs=in_specs, out_specs=out_specs, check_vma=False)
```

```python
import jax
import jax.numpy as jnp
from jax import lax
from jax.experimental import pallas as pl
from jax.experimental.pallas import tpu as pltpu
from jax.sharding import PartitionSpec as P

AXES = ("mod", "ex")
NT = (((1,), (1,)), ((), ()))
VMEM = 12 * 1024 * 1024


def pairs(x=0, yl=0, z=0, yh=0, c=0, only=None):
    out = []
    for mod in range(16):
        for ex in range(8):
            if only is not None and mod % 2 not in only:
                continue
            core = mod % 2
            dyh = yh[core] if isinstance(yh, tuple) else yh
            to_mod = ((mod // 4 + z) % 4) * 4 + ((mod // 2 % 2) ^ dyh) * 2 + (core ^ c)
            to_ex = ((ex // 4) ^ yl) * 4 + (ex % 4 + x) % 4
            out.append((mod * 8 + ex, to_mod * 8 + to_ex))
    return out


def move(a, **offset):
    return lax.ppermute(a, AXES, pairs(**offset))


def spread(top, low, whole, meanwhile=None):
    across = move(whole, yl=1)
    right_top, left_low = move(top, x=1), move(low, x=-1)
    right_low, left_top = move(low, x=1), move(top, x=-1)
    right_top, left_low, meanwhile = lax.optimization_barrier((right_top, left_low, meanwhile))
    far0, far1 = move(right_top, x=1), move(left_low, x=-1)
    across, right_low, left_top = lax.optimization_barrier((across, right_low, left_top))
    across_right, across_left = move(across, x=1), move(across, x=-1)
    corner0, corner1 = move(far0, yl=1), move(far1, yl=1)
    near = (top, low, right_top, right_low, left_top, left_low, across)
    return near, (far0, far1, across_right, across_left, corner0, corner1), meanwhile


def rows_of(blocks):
    return blocks[0][...] if len(blocks) == 1 else jnp.concatenate([b[...] for b in blocks], axis=0)


def on_chip(kernel, out_shape, scalars, *args):
    specs = [pl.BlockSpec(memory_space=pltpu.SMEM)] * len(scalars) + [pl.BlockSpec(memory_space=pltpu.VMEM)] * len(args)
    return pl.pallas_call(
        kernel,
        in_specs=specs,
        out_specs=jax.tree.map(lambda _: pl.BlockSpec(memory_space=pltpu.VMEM), out_shape),
        out_shape=out_shape,
        compiler_params=pltpu.CompilerParams(vmem_limit_bytes=VMEM),
        cost_estimate=pl.CostEstimate(flops=1, bytes_accessed=1, transcendentals=0),
    )(*scalars, *args)


def precondition(blocks, h):
    def kernel(*refs):
        *blocks, h, out = refs
        out[...] = lax.dot_general(rows_of(blocks), h[...], NT, preferred_element_type=jnp.float32).astype(out.dtype)

    rows = sum(b.shape[0] for b in blocks)
    return on_chip(kernel, jax.ShapeDtypeStruct((rows, 512), jnp.bfloat16), (), *blocks, h)


def precondition_order(blocks, h, first, place):
    def kernel(*refs):
        *blocks, h, first, place, top, low, whole = refs
        rest = lax.dot_general(rows_of(blocks), h[...], NT, preferred_element_type=jnp.float32).astype(top.dtype)
        both = jnp.concatenate([first[...], rest], axis=0)
        at = lax.broadcasted_iota(jnp.int32, (512, 512), 0)
        pick = (place[...] == at).astype(both.dtype)
        ordered = lax.dot_general(pick, both, (((0,), (0,)), ((), ())), preferred_element_type=jnp.float32)
        top[...] = ordered[:256].astype(top.dtype)
        low[...] = ordered[256:].astype(low.dtype)
        whole[...] = ordered.astype(low.dtype)

    half = jax.ShapeDtypeStruct((256, 512), jnp.bfloat16)
    return on_chip(kernel, [half, half, jax.ShapeDtypeStruct((512, 512), jnp.bfloat16)], (), *blocks, h, first, place)


def columns_of(slots, first, count, sketch, limit, top=None, low=None, held=None):
    total, tile = sketch.shape[0], 1024

    def kernel(slots, sketch, *refs):
        later, sems = refs[-2:]
        copies = [
            pltpu.make_async_copy(
                sketch.at[:, pl.ds(pl.multiple_of(slots[first + j] * 512, 512), 512)], later.at[j], sems.at[j]
            )
            for j in range(count)
        ]
        for copy in copies:
            copy.start()
        if top is not None:
            top_ref, low_ref, held_ref, out = refs[:4]
            rows = rows_of((top_ref, low_ref))
            for i in range(total // tile):
                at = slice(i * tile, i * tile + tile)
                out[:, at] = lax.dot_general(rows, held_ref[0, at], NT, preferred_element_type=jnp.float32)
        for copy in copies:
            copy.wait()

    smem, vmem = pl.BlockSpec(memory_space=pltpu.SMEM), pl.BlockSpec(memory_space=pltpu.VMEM)
    args = () if top is None else (top, low, held)
    out = [] if top is None else [jax.ShapeDtypeStruct((512, total), jnp.float32)]
    out += [jax.ShapeDtypeStruct((count, total, 512), jnp.bfloat16)]
    return pl.pallas_call(
        kernel,
        in_specs=[smem, pl.BlockSpec(memory_space=pl.ANY)] + [vmem] * len(args),
        out_specs=[vmem] * len(out),
        out_shape=out,
        scratch_shapes=[pltpu.SemaphoreType.DMA((count,))],
        compiler_params=pltpu.CompilerParams(vmem_limit_bytes=limit * 1024 * 1024),
        cost_estimate=pl.CostEstimate(flops=1, bytes_accessed=1, transcendentals=0),
    )(slots, sketch, *args)


def score_more(blocks, first, sketch, base, half=None, dtype=jnp.float32, tile=1024):
    total = sketch.shape[1]
    sizes = [len(b) for b in blocks]
    rows = 512 if half is None else 256

    def part(ref, columns=slice(None)):
        if ref.shape[0] == rows:
            return ref[:, columns]
        return ref[half * 256 : half * 256 + 256, columns]

    def kernel(*refs):
        held, (sketch, base, out) = list(refs[:-3]), refs[-3:]
        wholes = []
        for size in sizes:
            taken = [held.pop(0) for _ in range(size)]
            wholes.append(rows_of(taken) if size > 1 else part(taken[0]))
        for i in range(total // tile):
            at = slice(i * tile, i * tile + tile)
            terms = [
                lax.dot_general(w, sketch[first + j, at], NT, preferred_element_type=jnp.float32)
                for j, w in enumerate(wholes)
            ]
            out[:, at] = sum(terms, part(base, at)).astype(out.dtype)

    flat = [a for b in blocks for a in b]
    return on_chip(kernel, jax.ShapeDtypeStruct((rows, total), dtype), (), *flat, sketch, base)


def local(queries, hessian_inv, train_sketch, module_slot, arrival_of):
    mod, ex = lax.axis_index("mod"), lax.axis_index("ex")
    z, yh, c = mod // 4, mod // 2 % 2, mod % 2
    yl, x = ex // 4, ex % 4
    h, sketch = hessian_inv[0], train_sketch[:, 0]

    pick = (module_slot[:, None] == jnp.arange(16)[None, :]).astype(jnp.bfloat16)
    slotted = jnp.einsum("km,rmb->krb", pick, queries, preferred_element_type=jnp.float32).astype(jnp.bfloat16)
    own = lax.all_to_all(slotted, "mod", split_axis=0, concat_axis=0, tiled=True).reshape(64, 4096)

    arrival = arrival_of.reshape(4, 2, 2, 32)
    arrival = lax.dynamic_slice_in_dim(jnp.concatenate([arrival, arrival], axis=0), z, 4, axis=0)
    yhs = [jnp.where(yh == c, arrival[:, 1 - s], arrival[:, s]) for s in (0, 1)]
    row = jnp.stack([jnp.where(c == 0, yhs[s], yhs[s][:, ::-1]) for s in (0, 1)])
    row = jnp.stack([row[0], row[1][:, ::-1]]).reshape(1, 512)
    source = row // 4 % 8
    dx, dy = (source % 4 - x) % 4, (source // 4) ^ yl
    block = jnp.where(
        dy == 0,
        jnp.where(dx == 0, 0, jnp.where(dx == 3, 1, jnp.where(dx == 1, 2, 4))),
        jnp.where(dx == 0, 3, jnp.where(dx == 3, 5, jnp.where(dx == 1, 6, 7))),
    )
    place = block * 64 + (row // 32) * 4 + row % 4
    left, right, over = (x + 3) % 4, (x + 1) % 4, (x + 2) % 4
    here, there = yl * 4, (1 - yl) * 4
    slots = [here + x, here + left, here + right, there + x, here + over, there + left, there + right, there + over]
    own, place, slots = lax.optimization_barrier((own, place, jnp.stack(slots).astype(jnp.int32)))

    near, far, _ = spread(own[:32], own[32:], own)
    first = precondition(near, h)
    (now,) = columns_of(slots, 0, 5, sketch, 28)
    far, first, now = lax.optimization_barrier((far, first, now))
    top, low, whole = precondition_order(far, h, first, place)

    near, far, (base, later) = spread(top, low, whole, columns_of(slots, 5, 3, sketch, 28, top, low, now))
    _, _, right_top, right_low, left_top, left_low, across = near
    far0, far1, *far = far
    base = score_more(((right_top, right_low), (left_top, left_low), (across,), (far0, far1)), 1, now, base)
    across_right, across_left, corner0, corner1 = lax.optimization_barrier(far)
    send = score_more(((across_right,), (across_left,), (corner0,)), 0, later, base, 0, jnp.bfloat16)
    got = move(send, c=1)
    keep = score_more(((across_right,), (across_left,), (corner1,)), 0, later, base, 1)

    chip = keep + got.astype(jnp.float32)
    parts = chip.astype(jnp.bfloat16)
    arrived = [move(parts[64 * d : 64 * d + 64], z=d, yh=(0, 1)) for d in (1, 2, 3)]
    other = move(parts[:64], yh=(0, 1), only=(1,))
    total = jnp.where(c == 0, chip[:64], other.astype(jnp.float32))
    for a in arrived:
        total = total + a.astype(jnp.float32)
    return total[32:] + move(total[:32], c=1)


def solution(mesh):
    in_specs = (P(("mod", "ex"), None, None), P("mod", "ex", None), P("ex", "mod", None), P(), P())
    out_specs = P("mod", "ex")
    return jax.shard_map(local, mesh=mesh, in_specs=in_specs, out_specs=out_specs, check_vma=False)
```

```python
import jax
import jax.numpy as jnp
from jax import lax
from jax.experimental import pallas as pl
from jax.experimental.pallas import tpu as pltpu
from jax.sharding import PartitionSpec as P

AXES = ("mod", "ex")
NT = (((1,), (1,)), ((), ()))
VMEM = 12 * 1024 * 1024


def pairs(x=0, yl=0, z=0, yh=0, c=0, only=None):
    out = []
    for mod in range(16):
        for ex in range(8):
            if only is not None and mod % 2 not in only:
                continue
            core = mod % 2
            dyh = yh[core] if isinstance(yh, tuple) else yh
            to_mod = ((mod // 4 + z) % 4) * 4 + ((mod // 2 % 2) ^ dyh) * 2 + (core ^ c)
            to_ex = ((ex // 4) ^ yl) * 4 + (ex % 4 + (x if core == 0 else -x)) % 4
            out.append((mod * 8 + ex, to_mod * 8 + to_ex))
    return out


def move(a, **offset):
    return lax.ppermute(a, AXES, pairs(**offset))


def spread(top, low, whole, meanwhile=None):
    across = move(whole, yl=1)
    right_top, left_low = move(top, x=1), move(low, x=-1)
    right_low, left_top = move(low, x=1), move(top, x=-1)
    right_top, left_low, meanwhile = lax.optimization_barrier((right_top, left_low, meanwhile))
    far0, far1 = move(right_top, x=1), move(left_low, x=-1)
    across, right_low, left_top = lax.optimization_barrier((across, right_low, left_top))
    across_right, across_left = move(across, x=1), move(across, x=-1)
    corner0, corner1 = move(far0, yl=1), move(far1, yl=1)
    near = (top, low, right_top, right_low, left_top, left_low, across)
    return near, (far0, far1, across_right, across_left, corner0, corner1), meanwhile


def rows_of(blocks):
    return blocks[0][...] if len(blocks) == 1 else jnp.concatenate([b[...] for b in blocks], axis=0)


def on_chip(kernel, out_shape, scalars, *args):
    specs = [pl.BlockSpec(memory_space=pltpu.SMEM)] * len(scalars) + [pl.BlockSpec(memory_space=pltpu.VMEM)] * len(args)
    return pl.pallas_call(
        kernel,
        in_specs=specs,
        out_specs=jax.tree.map(lambda _: pl.BlockSpec(memory_space=pltpu.VMEM), out_shape),
        out_shape=out_shape,
        compiler_params=pltpu.CompilerParams(vmem_limit_bytes=VMEM),
        cost_estimate=pl.CostEstimate(flops=1, bytes_accessed=1, transcendentals=0),
    )(*scalars, *args)


def precondition(blocks, h):
    def kernel(*refs):
        *blocks, h, out = refs
        out[...] = lax.dot_general(rows_of(blocks), h[...], NT, preferred_element_type=jnp.float32).astype(out.dtype)

    rows = sum(b.shape[0] for b in blocks)
    return on_chip(kernel, jax.ShapeDtypeStruct((rows, 512), jnp.bfloat16), (), *blocks, h)


def precondition_order(blocks, h, first, place):
    def kernel(*refs):
        *blocks, h, first, place, top, low, whole = refs
        rest = lax.dot_general(rows_of(blocks), h[...], NT, preferred_element_type=jnp.float32).astype(top.dtype)
        both = jnp.concatenate([first[...], rest], axis=0)
        at = lax.broadcasted_iota(jnp.int32, (512, 512), 0)
        pick = (place[...] == at).astype(both.dtype)
        ordered = lax.dot_general(pick, both, (((0,), (0,)), ((), ())), preferred_element_type=jnp.float32)
        top[...] = ordered[:256].astype(top.dtype)
        low[...] = ordered[256:].astype(low.dtype)
        whole[...] = ordered.astype(low.dtype)

    half = jax.ShapeDtypeStruct((256, 512), jnp.bfloat16)
    return on_chip(kernel, [half, half, jax.ShapeDtypeStruct((512, 512), jnp.bfloat16)], (), *blocks, h, first, place)


def columns_of(slots, first, count, sketch, limit, top=None, low=None, held=None):
    total, tile = sketch.shape[0], 1024

    def kernel(slots, sketch, *refs):
        later, sems = refs[-2:]
        copies = [
            pltpu.make_async_copy(
                sketch.at[:, pl.ds(pl.multiple_of(slots[first + j] * 512, 512), 512)], later.at[j], sems.at[j]
            )
            for j in range(count)
        ]
        for copy in copies:
            copy.start()
        if top is not None:
            top_ref, low_ref, held_ref, out = refs[:4]
            rows = rows_of((top_ref, low_ref))
            for i in range(total // tile):
                at = slice(i * tile, i * tile + tile)
                out[:, at] = lax.dot_general(rows, held_ref[0, at], NT, preferred_element_type=jnp.float32)
        for copy in copies:
            copy.wait()

    smem, vmem = pl.BlockSpec(memory_space=pltpu.SMEM), pl.BlockSpec(memory_space=pltpu.VMEM)
    args = () if top is None else (top, low, held)
    out = [] if top is None else [jax.ShapeDtypeStruct((512, total), jnp.float32)]
    out += [jax.ShapeDtypeStruct((count, total, 512), jnp.bfloat16)]
    return pl.pallas_call(
        kernel,
        in_specs=[smem, pl.BlockSpec(memory_space=pl.ANY)] + [vmem] * len(args),
        out_specs=[vmem] * len(out),
        out_shape=out,
        scratch_shapes=[pltpu.SemaphoreType.DMA((count,))],
        compiler_params=pltpu.CompilerParams(vmem_limit_bytes=limit * 1024 * 1024),
        cost_estimate=pl.CostEstimate(flops=1, bytes_accessed=1, transcendentals=0),
    )(slots, sketch, *args)


def score_more(blocks, first, sketch, base, half=None, dtype=jnp.float32, tile=1024):
    total = sketch.shape[1]
    sizes = [len(b) for b in blocks]
    rows = 512 if half is None else 256

    def part(ref, columns=slice(None)):
        if ref.shape[0] == rows:
            return ref[:, columns]
        return ref[half * 256 : half * 256 + 256, columns]

    def kernel(*refs):
        held, (sketch, base, out) = list(refs[:-3]), refs[-3:]
        wholes = []
        for size in sizes:
            taken = [held.pop(0) for _ in range(size)]
            wholes.append(rows_of(taken) if size > 1 else part(taken[0]))
        for i in range(total // tile):
            at = slice(i * tile, i * tile + tile)
            terms = [
                lax.dot_general(w, sketch[first + j, at], NT, preferred_element_type=jnp.float32)
                for j, w in enumerate(wholes)
            ]
            out[:, at] = sum(terms, part(base, at)).astype(out.dtype)

    flat = [a for b in blocks for a in b]
    return on_chip(kernel, jax.ShapeDtypeStruct((rows, total), dtype), (), *flat, sketch, base)


def local(queries, hessian_inv, train_sketch, module_slot, arrival_of):
    mod, ex = lax.axis_index("mod"), lax.axis_index("ex")
    z, yh, c = mod // 4, mod // 2 % 2, mod % 2
    yl, x = ex // 4, ex % 4
    h, sketch = hessian_inv[0], train_sketch[:, 0]

    pick = (module_slot[:, None] == jnp.arange(16)[None, :]).astype(jnp.bfloat16)
    slotted = jnp.einsum("km,rmb->krb", pick, queries, preferred_element_type=jnp.float32).astype(jnp.bfloat16)
    own = lax.all_to_all(slotted, "mod", split_axis=0, concat_axis=0, tiled=True).reshape(64, 4096)

    arrival = arrival_of.reshape(4, 2, 2, 32)
    arrival = lax.dynamic_slice_in_dim(jnp.concatenate([arrival, arrival], axis=0), z, 4, axis=0)
    yhs = [jnp.where(yh == c, arrival[:, 1 - s], arrival[:, s]) for s in (0, 1)]
    row = jnp.stack([jnp.where(c == 0, yhs[s], yhs[s][:, ::-1]) for s in (0, 1)])
    row = jnp.stack([row[0], row[1][:, ::-1]]).reshape(1, 512)
    source = row // 4 % 8
    way = 1 - 2 * c
    dx, dy = (source % 4 - x) * way % 4, (source // 4) ^ yl
    block = jnp.where(
        dy == 0,
        jnp.where(dx == 0, 0, jnp.where(dx == 3, 1, jnp.where(dx == 1, 2, 4))),
        jnp.where(dx == 0, 3, jnp.where(dx == 3, 5, jnp.where(dx == 1, 6, 7))),
    )
    place = block * 64 + (row // 32) * 4 + row % 4
    left, right, over = (x - way) % 4, (x + way) % 4, (x + 2) % 4
    here, there = yl * 4, (1 - yl) * 4
    slots = [here + x, here + left, here + right, there + x, here + over, there + left, there + right, there + over]
    own, place, slots = lax.optimization_barrier((own, place, jnp.stack(slots).astype(jnp.int32)))

    near, far, _ = spread(own[:32], own[32:], own)
    first = precondition(near, h)
    (now,) = columns_of(slots, 0, 5, sketch, 28)
    far, first, now = lax.optimization_barrier((far, first, now))
    top, low, whole = precondition_order(far, h, first, place)

    near, far, (base, later) = spread(top, low, whole, columns_of(slots, 5, 3, sketch, 28, top, low, now))
    _, _, right_top, right_low, left_top, left_low, across = near
    far0, far1, *far = far
    base = score_more(((right_top, right_low), (left_top, left_low), (across,), (far0, far1)), 1, now, base)
    across_right, across_left, corner0, corner1 = lax.optimization_barrier(far)
    send = score_more(((across_right,), (across_left,), (corner0,)), 0, later, base, 0, jnp.bfloat16)
    got = move(send, c=1)
    keep = score_more(((across_right,), (across_left,), (corner1,)), 0, later, base, 1)

    chip = keep + got.astype(jnp.float32)
    parts = chip.astype(jnp.bfloat16)
    arrived = [move(parts[64 * d : 64 * d + 64], z=d, yh=(0, 1)) for d in (1, 2, 3)]
    other = move(parts[:64], yh=(0, 1), only=(1,))
    total = jnp.where(c == 0, chip[:64], other.astype(jnp.float32))
    for a in arrived:
        total = total + a.astype(jnp.float32)
    return total[32:] + move(total[:32], c=1)


def solution(mesh):
    in_specs = (P(("mod", "ex"), None, None), P("mod", "ex", None), P("ex", "mod", None), P(), P())
    out_specs = P("mod", "ex")
    return jax.shard_map(local, mesh=mesh, in_specs=in_specs, out_specs=out_specs, check_vma=False)
```

```python
import jax
import jax.numpy as jnp
from jax import lax
from jax.experimental import pallas as pl
from jax.experimental.pallas import tpu as pltpu
from jax.sharding import PartitionSpec as P

AXES = ("mod", "ex")
NT = (((1,), (1,)), ((), ()))
VMEM = 12 * 1024 * 1024


def pairs(x=0, yl=0, z=0, yh=0, c=0, only=None):
    out = []
    for mod in range(16):
        for ex in range(8):
            if only is not None and mod % 2 not in only:
                continue
            core = mod % 2
            dyh = yh[core] if isinstance(yh, tuple) else yh
            to_mod = ((mod // 4 + z) % 4) * 4 + ((mod // 2 % 2) ^ dyh) * 2 + (core ^ c)
            to_ex = ((ex // 4) ^ yl) * 4 + (ex % 4 + x) % 4
            out.append((mod * 8 + ex, to_mod * 8 + to_ex))
    return out


def move(a, **offset):
    return lax.ppermute(a, AXES, pairs(**offset))


def spread(top, low, whole, meanwhile=None):
    across = move(whole, yl=1)
    right_top, left_low = move(top, x=1), move(low, x=-1)
    right_low, left_top = move(low, x=1), move(top, x=-1)
    right_top, left_low, meanwhile = lax.optimization_barrier((right_top, left_low, meanwhile))
    far0, far1 = move(right_top, x=1), move(left_low, x=-1)
    across, right_low, left_top = lax.optimization_barrier((across, right_low, left_top))
    across_right, across_left = move(across, x=1), move(across, x=-1)
    corner0, corner1 = move(far0, yl=1), move(far1, yl=1)
    near = (top, low, right_top, right_low, left_top, left_low, across)
    return near, (far0, far1, across_right, across_left, corner0, corner1), meanwhile


def rows_of(blocks):
    return blocks[0][...] if len(blocks) == 1 else jnp.concatenate([b[...] for b in blocks], axis=0)


def on_chip(kernel, out_shape, scalars, *args):
    specs = [pl.BlockSpec(memory_space=pltpu.SMEM)] * len(scalars) + [pl.BlockSpec(memory_space=pltpu.VMEM)] * len(args)
    return pl.pallas_call(
        kernel,
        in_specs=specs,
        out_specs=jax.tree.map(lambda _: pl.BlockSpec(memory_space=pltpu.VMEM), out_shape),
        out_shape=out_shape,
        compiler_params=pltpu.CompilerParams(vmem_limit_bytes=VMEM),
        cost_estimate=pl.CostEstimate(flops=1, bytes_accessed=1, transcendentals=0),
    )(*scalars, *args)


def precondition(blocks, h):
    def kernel(*refs):
        *blocks, h, out = refs
        out[...] = lax.dot_general(rows_of(blocks), h[...], NT, preferred_element_type=jnp.float32).astype(out.dtype)

    rows = sum(b.shape[0] for b in blocks)
    return on_chip(kernel, jax.ShapeDtypeStruct((rows, 512), jnp.bfloat16), (), *blocks, h)


def precondition_order(blocks, h, first, place):
    def kernel(*refs):
        *blocks, h, first, place, top, low, whole = refs
        rest = lax.dot_general(rows_of(blocks), h[...], NT, preferred_element_type=jnp.float32).astype(top.dtype)
        both = jnp.concatenate([first[...], rest], axis=0)
        at = lax.broadcasted_iota(jnp.int32, (512, 512), 0)
        pick = (place[...] == at).astype(both.dtype)
        ordered = lax.dot_general(pick, both, (((0,), (0,)), ((), ())), preferred_element_type=jnp.float32)
        top[...] = ordered[:256].astype(top.dtype)
        low[...] = ordered[256:].astype(low.dtype)
        whole[...] = ordered.astype(low.dtype)

    half = jax.ShapeDtypeStruct((256, 512), jnp.bfloat16)
    return on_chip(kernel, [half, half, jax.ShapeDtypeStruct((512, 512), jnp.bfloat16)], (), *blocks, h, first, place)


def columns_of(slots, first, count, sketch, limit, top=None, low=None, held=None):
    total, tile = sketch.shape[0], 1024

    def kernel(slots, sketch, *refs):
        later, sems = refs[-2:]
        copies = [
            pltpu.make_async_copy(
                sketch.at[:, pl.ds(pl.multiple_of(slots[first + j] * 512, 512), 512)], later.at[j], sems.at[j]
            )
            for j in range(count)
        ]
        for copy in copies:
            copy.start()
        if top is not None:
            top_ref, low_ref, held_ref, out = refs[:4]
            rows = rows_of((top_ref, low_ref))
            for i in range(total // tile):
                at = slice(i * tile, i * tile + tile)
                out[:, at] = lax.dot_general(rows, held_ref[0, at], NT, preferred_element_type=jnp.float32)
        for copy in copies:
            copy.wait()

    smem, vmem = pl.BlockSpec(memory_space=pltpu.SMEM), pl.BlockSpec(memory_space=pltpu.VMEM)
    args = () if top is None else (top, low, held)
    out = [] if top is None else [jax.ShapeDtypeStruct((512, total), jnp.float32)]
    out += [jax.ShapeDtypeStruct((count, total, 512), jnp.bfloat16)]
    return pl.pallas_call(
        kernel,
        in_specs=[smem, pl.BlockSpec(memory_space=pl.ANY)] + [vmem] * len(args),
        out_specs=[vmem] * len(out),
        out_shape=out,
        scratch_shapes=[pltpu.SemaphoreType.DMA((count,))],
        compiler_params=pltpu.CompilerParams(vmem_limit_bytes=limit * 1024 * 1024),
        cost_estimate=pl.CostEstimate(flops=1, bytes_accessed=1, transcendentals=0),
    )(slots, sketch, *args)


def score_more(blocks, first, sketch, base, half=None, dtype=jnp.float32, tile=1024):
    total = sketch.shape[1]
    sizes = [len(b) for b in blocks]
    rows = 512 if half is None else 256

    def part(ref, columns=slice(None)):
        if ref.shape[0] == rows:
            return ref[:, columns]
        return ref[half * 256 : half * 256 + 256, columns]

    def kernel(*refs):
        held, (sketch, base, out) = list(refs[:-3]), refs[-3:]
        wholes = []
        for size in sizes:
            taken = [held.pop(0) for _ in range(size)]
            wholes.append(rows_of(taken) if size > 1 else part(taken[0]))
        for i in range(total // tile):
            at = slice(i * tile, i * tile + tile)
            terms = [
                lax.dot_general(w, sketch[first + j, at], NT, preferred_element_type=jnp.float32)
                for j, w in enumerate(wholes)
            ]
            out[:, at] = sum(terms, part(base, at)).astype(out.dtype)

    flat = [a for b in blocks for a in b]
    return on_chip(kernel, jax.ShapeDtypeStruct((rows, total), dtype), (), *flat, sketch, base)


def local(queries, hessian_inv, train_sketch, module_slot, arrival_of):
    mod, ex = lax.axis_index("mod"), lax.axis_index("ex")
    z, yh, c = mod // 4, mod // 2 % 2, mod % 2
    yl, x = ex // 4, ex % 4
    h, sketch = hessian_inv[0], train_sketch[:, 0]

    pick = (module_slot[:, None] == jnp.arange(16)[None, :]).astype(jnp.bfloat16)
    slotted = jnp.einsum("km,rmb->krb", pick, queries, preferred_element_type=jnp.float32).astype(jnp.bfloat16)
    own = lax.all_to_all(slotted, "mod", split_axis=0, concat_axis=0, tiled=True).reshape(64, 4096)

    arrival = arrival_of.reshape(4, 2, 2, 32)
    arrival = lax.dynamic_slice_in_dim(jnp.concatenate([arrival, arrival], axis=0), z, 4, axis=0)
    yhs = [jnp.where(yh == c, arrival[:, 1 - s], arrival[:, s]) for s in (0, 1)]
    row = jnp.stack([jnp.where(c == 0, yhs[s], yhs[s][:, ::-1]) for s in (0, 1)])
    row = jnp.stack([row[0], row[1][:, ::-1]]).reshape(1, 512)
    source = row // 4 % 8
    dx, dy = (source % 4 - x) % 4, (source // 4) ^ yl
    block = jnp.where(
        dy == 0,
        jnp.where(dx == 0, 0, jnp.where(dx == 3, 1, jnp.where(dx == 1, 2, 4))),
        jnp.where(dx == 0, 3, jnp.where(dx == 3, 5, jnp.where(dx == 1, 6, 7))),
    )
    place = block * 64 + (row // 32) * 4 + row % 4
    left, right, over = (x + 3) % 4, (x + 1) % 4, (x + 2) % 4
    here, there = yl * 4, (1 - yl) * 4
    slots = [here + x, here + left, here + right, there + x, here + over, there + left, there + right, there + over]
    own, place, slots = lax.optimization_barrier((own, place, jnp.stack(slots).astype(jnp.int32)))

    near, far, now = spread(own[:32], own[32:], own, columns_of(slots, 0, 5, sketch, 28)[0])
    first = precondition(near, h)
    top, low, whole = precondition_order(far, h, first, place)

    near, far, (base, later) = spread(top, low, whole, columns_of(slots, 5, 3, sketch, 28, top, low, now))
    _, _, right_top, right_low, left_top, left_low, across = near
    far0, far1, *far = far
    base = score_more(((right_top, right_low), (left_top, left_low), (across,), (far0, far1)), 1, now, base)
    across_right, across_left, corner0, corner1 = lax.optimization_barrier(far)
    send = score_more(((across_right,), (across_left,), (corner0,)), 0, later, base, 0, jnp.bfloat16)
    got = move(send, c=1)
    keep = score_more(((across_right,), (across_left,), (corner1,)), 0, later, base, 1)

    chip = keep + got.astype(jnp.float32)
    parts = chip.astype(jnp.bfloat16)
    arrived = [move(parts[64 * d : 64 * d + 64], z=d, yh=(0, 1)) for d in (1, 2, 3)]
    other = move(parts[:64], yh=(0, 1), only=(1,))
    total = jnp.where(c == 0, chip[:64], other.astype(jnp.float32))
    for a in arrived:
        total = total + a.astype(jnp.float32)
    return total[32:] + move(total[:32], c=1)


def solution(mesh):
    in_specs = (P(("mod", "ex"), None, None), P("mod", "ex", None), P("ex", "mod", None), P(), P())
    out_specs = P("mod", "ex")
    return jax.shard_map(local, mesh=mesh, in_specs=in_specs, out_specs=out_specs, check_vma=False)
```
